32 devices in a mesh: groups: 2 (over x), rows: 16 (over z, y, core).
Axes of the slice: x: 2, y: 2, z: 4, core: 2. Of those that a mesh axis runs over, the one named last changes fastest.
Arguments:
- image_query: bfloat16 [12288, 2048], P(('groups', 'rows')), parts along dimension 0, may hold values from -40 to 40
- image_pairs: bfloat16 [2, 12288, 2048], P(None, ('groups', 'rows')), parts along dimension 1, may hold values from -6 to 6
- text_query: bfloat16 [512, 2048], P(('groups', 'rows')), parts along dimension 0, may hold values from -40 to 40
- text_pairs: bfloat16 [2, 512, 2048], P(None, ('groups', 'rows')), parts along dimension 1, may hold values from -6 to 6
- text_mask: int32 [512], P('groups'), parts along dimension 0, may hold values 0 or 1
- window_offsets: int32 [16, 2], replicated, may hold values from -1 to 1, as said below
- timestep: int32 [1], replicated, may hold values from 0 to 49
- gate_table: float32 [50, 2, 2048], replicated, may hold values from 0.5 to 2
Outputs:
- image_out: bfloat16 [12288, 2048], P(('groups', 'rows')), parts along dimension 0
- text_out: bfloat16 [512, 2048], P(('groups', 'rows')), parts along dimension 0
The draws below stay inside these ranges and needn't reach their ends.
There are 2 independent parts, one for each index of `groups`. The reference program is written for one: setup_inputs(seed, part) draws one part's arguments, and reference() takes and returns one part's arrays. A program takes and returns all parts, laid end to end along the dimension named above; an argument that names none is the same for every part. Nothing has to cross between parts.
Inputs may be any that keep to these rules, and one draw needn't show every extreme that they name: window_offsets[h, 0] is -1 or 0 and window_offsets[h, 1] is 0 or 1; some head has -1 and some head has 1.
All inputs are finite; a program needn't handle non-finite values.
Results may differ from the reference program's by a relative error of at most 0.02.
Values may be sent and summed in bfloat16 or wider, within the bound.
A program may use at most 128 MiB of HBM per device.

```python
import math
import jax
import jax.numpy as jnp
from jax import lax

HEADS = 16
HEAD = 128
TILE = 384
TILES_DEV = 1
TEXT = 256
STEPS = 50
D = 2048
TILES = 16
PIX = 6144


def draw_image_pairs(key, part):
    sample = jnp.clip(jax.random.normal(jax.random.fold_in(key, 1), (2, PIX, D)), -6.0, 6.0)
    return sample.astype(jnp.bfloat16)


def draw_image_query(key, part):
    sample = jnp.clip(2.0 * jax.random.normal(jax.random.fold_in(key, 2), (PIX, D)), -8.0, 8.0)
    return sample.astype(jnp.bfloat16)


def draw_text_query(key, part):
    sample = jnp.clip(3.5 * jax.random.normal(jax.random.fold_in(key, 3), (TEXT, D)), -14.0, 14.0)
    return sample.astype(jnp.bfloat16)


def draw_text_pairs(key, part):
    sample = jnp.clip(jax.random.normal(jax.random.fold_in(key, 4), (2, TEXT, D)), -6.0, 6.0)
    return sample.astype(jnp.bfloat16)


def draw_window_offsets(key, part):
    reach_back = -jax.random.randint(jax.random.fold_in(key, 21), (HEADS,), 0, 2)
    reach_ahead = jax.random.randint(jax.random.fold_in(key, 22), (HEADS,), 0, 2)
    ordering = jax.random.permutation(jax.random.fold_in(key, 23), HEADS)
    reach_back = reach_back.at[ordering[0]].set(-1)
    reach_ahead = reach_ahead.at[ordering[1]].set(1)
    return jnp.stack([reach_back, reach_ahead], axis=1).astype(jnp.int32)


def touch_ends(array, rng, least, high):
    place = [jax.random.randint(jax.random.fold_in(rng, axis), (), 0, length) for axis, length in enumerate(array.shape)]
    widest = array.shape.index(max(array.shape))
    neighbour = place[:widest] + [(place[widest] + 1) % array.shape[widest]] + place[widest + 1:]
    return array.at[tuple(place)].set(least).at[tuple(neighbour)].set(high)


def setup_inputs(seed: int = 0, part: int = 0) -> dict:
    seeds = jax.random.split(jax.random.key(seed), 9)
    own_keys = jax.random.split(jax.random.fold_in(seeds[8], part), 9)
    image_query = draw_image_query(jax.random.fold_in(jax.random.fold_in(seeds[8], part), 71), part)
    image_pairs = draw_image_pairs(jax.random.fold_in(jax.random.fold_in(seeds[8], part), 71), part)
    text_query = draw_text_query(jax.random.fold_in(jax.random.fold_in(seeds[8], part), 71), part)
    text_pairs = draw_text_pairs(jax.random.fold_in(jax.random.fold_in(seeds[8], part), 71), part)
    text_mask = touch_ends((jax.random.randint(own_keys[4], (TEXT,), 0, 4) < 3).astype(jnp.int32), jax.random.fold_in(own_keys[4], 1), 0, 1)
    window_offsets = draw_window_offsets(jax.random.fold_in(seeds[8], 71), part)
    timestep = jax.random.randint(seeds[6], (1,), 0, STEPS).astype(jnp.int32)
    gate_table = jnp.clip(jnp.exp(jax.random.uniform(seeds[7], (STEPS, 2, D), jnp.float32, math.log(0.5), math.log(2.0))), 0.5, 2.0)
    return {"image_query": image_query, "image_pairs": image_pairs, "text_query": text_query, "text_pairs": text_pairs, "text_mask": text_mask, "window_offsets": window_offsets, "timestep": timestep, "gate_table": gate_table}


masked_score = -1e+30

def attend_rows(queries, key_rows, value_rows, allowed, scaling):
    scores = jnp.einsum('qhe,khe->qhk', queries.astype(jnp.float32), key_rows.astype(jnp.float32)) * scaling
    scores = jnp.where(allowed, scores, masked_score)
    maxima = lax.optimization_barrier(jnp.max(scores, axis=-1))
    exponent = jnp.where(allowed, jnp.exp(scores - maxima[..., None]), 0.0)
    totals = lax.optimization_barrier(jnp.sum(exponent, axis=-1))
    weights = lax.optimization_barrier(exponent.astype(jnp.bfloat16)).astype(jnp.float32)
    summed = jnp.einsum('qhk,khe->qhe', weights, value_rows.astype(jnp.float32))
    summed = lax.optimization_barrier(summed.astype(jnp.bfloat16)).astype(jnp.float32)
    return (maxima, totals, summed)

def merge_parts(former, latter):
    largest = jnp.maximum(former[0], latter[0])
    former_scale = jnp.exp(former[0] - largest)
    latter_scale = jnp.exp(latter[0] - largest)
    return (largest, former[1] * former_scale + latter[1] * latter_scale, former[2] * former_scale[..., None] + latter[2] * latter_scale[..., None])

def combine_groups(groups):
    largest = groups[0][0]
    for member in groups[1:]:
        largest = jnp.maximum(largest, member[0])
    totals = 0.0
    summed = 0.0
    for member in groups:
        factor = jnp.exp(member[0] - largest)
        totals = totals + member[1] * factor
        summed = summed + member[2] * factor[..., None]
    return summed / totals[..., None]

def reference(image_query, image_pairs, text_query, text_pairs, text_mask, window_offsets, timestep, gate_table):
    scaling = 1.0 / math.sqrt(HEAD)
    queries = image_query.reshape(TILES, TILE, HEADS, HEAD)
    key_tiles = image_pairs[0].reshape(TILES, TILE, HEADS, HEAD)
    value_tiles = image_pairs[1].reshape(TILES, TILE, HEADS, HEAD)
    text_keys = text_pairs[0].reshape(TEXT, HEADS, HEAD)
    text_values = text_pairs[1].reshape(TEXT, HEADS, HEAD)
    text_allowed = (text_mask == 1)[None, None, :]
    reach_back = window_offsets[:, 0]
    reach_ahead = window_offsets[:, 1]
    gate_rows = lax.dynamic_index_in_dim(gate_table, timestep[0].astype(jnp.int32), 0, keepdims=False)

    def one_tile(index):
        tile_queries = queries[index]
        groups = [attend_rows(tile_queries, text_keys, text_values, text_allowed, scaling)]
        for offset in (-1, 0, 1):
            target = index + offset
            inside = (target >= 0) & (target < TILES)
            clamped = jnp.clip(target, 0, TILES - 1).astype(jnp.int32)
            allowed = (inside & (reach_back <= offset) & (offset <= reach_ahead))[None, :, None]
            groups.append(attend_rows(tile_queries, key_tiles[clamped], value_tiles[clamped], allowed, scaling))
        return combine_groups(groups)
    attended = lax.map(one_tile, jnp.arange(TILES, dtype=jnp.int32))
    image_out = (attended.reshape(PIX, D) * gate_rows[0]).astype(jnp.bfloat16)
    slab_rows = TILES_DEV * TILE
    text_flat = text_query.reshape(TEXT, HEADS, HEAD)
    all_keys = jnp.ones((1, 1, slab_rows), dtype=bool)

    def slab_step(carry, index):
        start = (index * slab_rows).astype(jnp.int32)
        slab_keys = lax.dynamic_slice_in_dim(image_pairs[0], start, slab_rows, 0).reshape(slab_rows, HEADS, HEAD)
        slab_values = lax.dynamic_slice_in_dim(image_pairs[1], start, slab_rows, 0).reshape(slab_rows, HEADS, HEAD)
        member = attend_rows(text_flat, slab_keys, slab_values, all_keys, scaling)
        return (merge_parts(carry, member), None)
    initial = (jnp.full((TEXT, HEADS), masked_score, jnp.float32), jnp.zeros((TEXT, HEADS), jnp.float32), jnp.zeros((TEXT, HEADS, HEAD), jnp.float32))
    carried, _ = lax.scan(slab_step, initial, jnp.arange(TILES // TILES_DEV, dtype=jnp.int32))
    own_text = attend_rows(text_flat, text_keys, text_values, text_allowed, scaling)
    text_attended = combine_groups([carried, own_text])
    text_out = (text_attended.reshape(TEXT, D) * gate_rows[1]).astype(jnp.bfloat16)
    return (image_out, text_out)
```

```python
import functools
import math

import jax
import jax.numpy as jnp
from jax import lax
from jax.experimental import pallas as pl
from jax.experimental.pallas import tpu as pltpu
from jax.sharding import PartitionSpec as P

TILE = 384


masked_score = -1e30


def extended_2(cells, sides, width):
    for axis, dim in sides:
        count = lax.axis_size(axis)
        ends = count - 1
        head = lax.slice_in_dim(cells, 0, width, axis=dim)
        tail = lax.slice_in_dim(cells, cells.shape[dim] - width, cells.shape[dim], axis=dim)
        cells = jnp.concatenate(
            [
                lax.ppermute(tail, axis, [(i, (i + 1) % count) for i in range(ends)]),
                cells,
                lax.ppermute(head, axis, [((i + 1) % count, i) for i in range(ends)]),
            ],
            axis=dim,
        )
    return cells


def attend_tiles(queries, key_rows, value_rows, allowed, scaling):
    scores = (
        jnp.einsum("tqhe,tkhe->tqhk", queries, key_rows, preferred_element_type=jnp.float32)
        * scaling
    )
    scores = jnp.where(allowed, scores, masked_score)
    maxima = jnp.max(scores, axis=-1)
    exponent = jnp.where(allowed, jnp.exp(scores - maxima[..., None]), 0.0)
    totals = jnp.sum(exponent, axis=-1)
    summed = jnp.einsum(
        "tqhk,tkhe->tqhe",
        exponent.astype(jnp.bfloat16),
        value_rows,
        preferred_element_type=jnp.float32,
    )
    return (maxima, totals, summed.astype(jnp.bfloat16))


def attend_rows(queries, key_rows, value_rows, allowed, scaling):
    scores = (
        jnp.einsum("qhe,khe->qhk", queries, key_rows, preferred_element_type=jnp.float32) * scaling
    )
    scores = jnp.where(allowed, scores, masked_score)
    maxima = jnp.max(scores, axis=-1)
    exponent = jnp.where(allowed, jnp.exp(scores - maxima[..., None]), 0.0)
    totals = jnp.sum(exponent, axis=-1)
    summed = jnp.einsum(
        "qhk,khe->qhe",
        exponent.astype(jnp.bfloat16),
        value_rows,
        preferred_element_type=jnp.float32,
    )
    return (maxima, totals, summed.astype(jnp.bfloat16))


def combine_groups(groups):
    largest = groups[0][0]
    for member in groups[1:]:
        largest = jnp.maximum(largest, member[0])
    totals = 0.0
    summed = 0.0
    for member in groups:
        factor = jnp.exp(member[0] - largest)
        totals = totals + member[1] * factor
        summed = summed + member[2].astype(jnp.float32) * factor[..., None]
    return summed / totals[..., None]


def on_device(
    image_query,
    image_pairs,
    text_query,
    text_pairs,
    text_mask,
    window_offsets,
    timestep,
    gate_table,
):
    rows_dev, width = image_query.shape
    tiles_dev = rows_dev // TILE
    head_count = window_offsets.shape[0]
    head_width = width // head_count
    scaling = 1.0 / math.sqrt(head_width)
    position = lax.axis_index("rows")
    tiles_all = tiles_dev * lax.axis_size("rows")
    first_tile = position * tiles_dev
    reach_back = window_offsets[:, 0]
    reach_ahead = window_offsets[:, 1]
    text_queries, text_gathered = (
        lax.all_gather(text_query, "rows", axis=0, tiled=True),
        lax.all_gather(text_pairs, "rows", axis=1, tiled=True),
    )
    text_keys = text_gathered[0].reshape(-1, head_count, head_width)
    text_values = text_gathered[1].reshape(-1, head_count, head_width)
    text_allowed = (text_mask == 1)[None, None, :]
    queries = image_query.reshape(tiles_dev, TILE, head_count, head_width)
    local_keys = image_pairs[0].reshape(tiles_dev, TILE, head_count, head_width)
    local_values = image_pairs[1].reshape(tiles_dev, TILE, head_count, head_width)

    def permitted(offset):
        target = first_tile + jnp.arange(tiles_dev, dtype=jnp.int32) + offset
        inside = (target >= 0) & (target < tiles_all)
        within = (reach_back <= offset) & (offset <= reach_ahead)
        return (inside[:, None] & within[None, :])[:, None, :, None]

    flat_queries = image_query.reshape(rows_dev, head_count, head_width)
    text_group = attend_rows(flat_queries, text_keys, text_values, text_allowed, scaling)
    text_group = (
        text_group[0].reshape(tiles_dev, TILE, head_count),
        text_group[1].reshape(tiles_dev, TILE, head_count),
        text_group[2].reshape(tiles_dev, TILE, head_count, head_width),
    )
    groups = [attend_tiles(queries, local_keys, local_values, permitted(0), scaling), text_group]
    extended = extended_2(image_pairs, (("rows", 1),), TILE)
    extended = extended.reshape(2, tiles_dev + 2, TILE, head_count, head_width)
    for offset in (-1, 1):
        groups.append(
            attend_tiles(
                queries,
                extended[0, 1 + offset : 1 + offset + tiles_dev],
                extended[1, 1 + offset : 1 + offset + tiles_dev],
                permitted(offset),
                scaling,
            )
        )
    gate_rows = lax.dynamic_index_in_dim(gate_table, timestep[0], 0, keepdims=False)
    attended = combine_groups(groups).reshape(rows_dev, width)
    image_out = (attended * gate_rows[0]).astype(jnp.bfloat16)
    text_flat = text_queries.reshape(-1, head_count, head_width)
    image_keys = image_pairs[0].reshape(rows_dev, head_count, head_width)
    image_values = image_pairs[1].reshape(rows_dev, head_count, head_width)
    every_key = jnp.ones((1, 1, rows_dev), dtype=bool)
    maxima, totals, summed = attend_rows(text_flat, image_keys, image_values, every_key, scaling)
    text_dev = text_query.shape[0]
    text_start = position * text_dev
    global_max = lax.pmax(maxima, "rows")
    factor = jnp.exp(maxima - global_max)
    scaled_summed = summed.astype(jnp.float32) * factor[..., None]
    scaled_totals = totals * factor
    whole_summed, whole_totals = lax.psum((scaled_summed, scaled_totals), "rows")
    shared_summed = lax.dynamic_slice_in_dim(whole_summed, text_start, text_dev, 0)
    shared_totals = lax.dynamic_slice_in_dim(whole_totals, text_start, text_dev, 0)
    remote = (
        lax.dynamic_slice_in_dim(global_max, text_start, text_dev, 0),
        shared_totals,
        shared_summed,
    )
    own_rows = text_query.reshape(text_dev, head_count, head_width)
    own_text = attend_rows(own_rows, text_keys, text_values, text_allowed, scaling)
    text_attended = combine_groups([remote, own_text]).reshape(text_dev, width)
    text_out = (text_attended * gate_rows[1]).astype(jnp.bfloat16)
    return (image_out, text_out)


CAPS = (11,)
MESH = pl.DeviceIdType.MESH


def flipped(pos, bits):
    out = pos
    bit = 1
    while bit <= bits:
        if bits & bit:
            out = out + bit - 2 * bit * ((pos // bit) % 2)
        bit *= 2
    return out


def stage_bits(count):
    bits = []
    bit = count // 2
    while bit >= 1:
        bits.append(bit)
        bit //= 2
    if len(bits) == 4:
        bits = [bits[0], bits[2], bits[1], bits[3]]
    return bits


def joint_kernel(
    count,
    slots,
    heads,
    scale2,
    table,
    q_ref,
    pairs_ref,
    tq_ref,
    tp_ref,
    bias_ref,
    gate_ref,
    out_ref,
    tout_ref,
    hq,
    hkv,
    packed,
    landed,
    tq_all,
    tkv_all,
    part_o,
    part_ml,
    stat,
    o_send,
    o_recv,
    s_send,
    s_recv,
    gs_sem,
    gr_sem,
    hs_sem,
    hr_sem,
    as_sem,
    ar_sem,
):
    pos = lax.axis_index("rows")
    grp = lax.axis_index("groups")
    rows = q_ref.shape[0]
    tdev = tq_ref.shape[0]
    text = count * tdev
    width = q_ref.shape[1] // heads

    barrier = pltpu.get_barrier_semaphore()

    def greet(d, _):
        pl.semaphore_signal(
            barrier, inc=1, device_id=(grp, lax.rem(pos + d, count)), device_id_type=MESH
        )
        return 0

    lax.fori_loop(1, count, greet, 0)
    pl.semaphore_wait(barrier, count - 1)

    def cols(h):
        return pl.ds(pl.multiple_of(h * width, width), width)

    bits = stage_bits(count)
    refs = (tq_all, tkv_all)

    def gather_copy(kind, number, block, partner):
        ref = tq_all.at[block] if kind == 0 else tkv_all.at[:, block]
        return pltpu.make_async_remote_copy(
            src_ref=ref,
            dst_ref=ref,
            send_sem=gs_sem.at[kind, number],
            recv_sem=gr_sem.at[kind, number],
            device_id=(grp, partner),
            device_id_type=MESH,
        )

    plan = []
    offsets = [0]
    number = 0
    for bit in bits:
        stage = []
        for off in offsets:
            stage.append((number, off, bit))
            number += 1
        plan.append(stage)
        offsets = offsets + [off ^ bit for off in offsets]

    def gather_start(kind, stage):
        for num, off, bit in plan[stage]:
            gather_copy(kind, num, flipped(pos, off), flipped(pos, bit)).start()

    def gather_land(kind, stage):
        for num, off, bit in plan[stage]:
            gather_copy(kind, num, flipped(pos, off ^ bit), flipped(pos, bit)).wait_recv()

    def gather_sent(kind, stage):
        for num, off, bit in plan[stage]:
            gather_copy(kind, num, flipped(pos, off), flipped(pos, bit)).wait_send()

    tq_all[pos] = tq_ref[...]
    tkv_all[:, pos] = tp_ref[...]
    gather_start(0, 0)
    gather_start(1, 0)

    def halo_copy(side, j):
        partner = pos + 1 if side == 0 else pos - 1
        return pltpu.make_async_remote_copy(
            src_ref=packed.at[side, j],
            dst_ref=landed.at[side, j],
            send_sem=hs_sem.at[side, j],
            recv_sem=hr_sem.at[side, j],
            device_id=(grp, partner),
            device_id_type=MESH,
        )

    has_prev = pos > 0
    has_next = pos < count - 1

    for h in range(heads):
        at = slice(h * width, (h + 1) * width)
        hkv[h] = pairs_ref[:, :, at]
        hq[h] = q_ref[:, at]

    def pack(j, _):
        @pl.when(has_next)
        def _():
            h = table[0, j]
            packed[0, j] = hkv[h]
            halo_copy(0, j).start()

        @pl.when(has_prev)
        def _():
            h = table[1, j]
            packed[1, j] = hkv[h]
            halo_copy(1, j).start()

        return 0

    lax.fori_loop(0, slots, pack, 0)

    def partial(keys, values, queries, bias):
        scores = lax.dot_general(
            keys, queries, (((1,), (1,)), ((), ())), preferred_element_type=jnp.float32
        )
        if bias is not None:
            scores = scores + bias
        top = jnp.max(scores, axis=0, keepdims=True)
        weights = jnp.exp2((scores - top) * scale2)
        total = jnp.sum(weights, axis=0, keepdims=True)
        summed = lax.dot_general(
            values,
            weights.astype(jnp.bfloat16),
            (((0,), (0,)), ((), ())),
            preferred_element_type=jnp.float32,
        )
        return top, total, summed

    def keep(kind, j, result):
        top, total, summed = result
        part_o[kind, j] = summed
        part_ml[kind, j, 0:1, :] = top
        part_ml[kind, j, 1:2, :] = total

    def local_head(h, _):
        keep(
            0,
            h,
            partial(hkv[h, 0], hkv[h, 1], hq[h], None),
        )
        return 0

    stages = len(bits)
    done = 0
    for stage in range(stages):
        upto = heads * (stage + 1) // stages
        lax.fori_loop(done, upto, local_head, 0)
        done = upto
        for kind in (0, 1):
            gather_land(kind, stage)
            if stage + 1 < stages:
                gather_start(kind, stage + 1)

    stat[...] = jnp.zeros_like(stat)
    own_bias = bias_ref[pl.ds(pl.multiple_of(pos * tdev, tdev), tdev), 0:1]
    slab_bias = jnp.concatenate([jnp.zeros((rows, 1), jnp.float32), own_bias], axis=0)

    def text_head(h, _):
        keys = jnp.concatenate([hkv[h, 0], tp_ref[0, :, cols(h)]], axis=0)
        values = jnp.concatenate([hkv[h, 1], tp_ref[1, :, cols(h)]], axis=0)
        queries = tq_all[:, :, cols(h)].reshape(text, width)
        top, total, summed = partial(keys, values, queries, slab_bias)
        stat[0, pl.ds(h, 1), :] = top
        stat[1, pl.ds(h, 1), :] = total
        o_send[:, :, cols(h)] = summed.T.astype(jnp.bfloat16).reshape(count, tdev, width)
        return 0

    lax.fori_loop(0, heads, text_head, 0)
    s_send[:, 0] = stat[0].T.reshape(count, tdev, 128)
    s_send[:, 1] = stat[1].T.reshape(count, tdev, 128)

    def spread_copy(kind, d, source, target):
        send, recv = ((o_send, o_recv), (s_send, s_recv))[kind]
        return pltpu.make_async_remote_copy(
            src_ref=send.at[target],
            dst_ref=recv.at[source],
            send_sem=as_sem.at[kind, d],
            recv_sem=ar_sem.at[kind, d],
            device_id=(grp, target),
            device_id_type=MESH,
        )

    def spread_start(d, _):
        target = lax.rem(pos + d, count)
        spread_copy(0, d, pos, target).start()
        spread_copy(1, d, pos, target).start()
        return 0

    lax.fori_loop(1, count, spread_start, 0)
    o_recv[pos] = o_send[pos]
    s_recv[pos] = s_send[pos]

    def image_text(h, _):
        keys = tkv_all[0, :, :, cols(h)].reshape(text, width)
        values = tkv_all[1, :, :, cols(h)].reshape(text, width)
        keep(1, h, partial(keys, values, hq[h], bias_ref[:, 0:1]))
        return 0

    lax.fori_loop(0, heads, image_text, 0)

    def halo_head(j, _):
        @pl.when(has_prev)
        def _():
            halo_copy(0, j).wait_recv()
            queries = hq[table[0, j]]
            keep(2, j, partial(landed[0, j, 0], landed[0, j, 1], queries, None))

        @pl.when(has_next)
        def _():
            halo_copy(1, j).wait_recv()
            queries = hq[table[1, j]]
            keep(3, j, partial(landed[1, j, 0], landed[1, j, 1], queries, None))

        return 0

    lax.fori_loop(0, slots, halo_head, 0)

    prev_i = jnp.where(has_prev, 1, 0)
    next_i = jnp.where(has_next, 1, 0)

    def finish(h, _):
        slot_p, slot_n = table[2, h], table[3, h]
        use_p = jnp.full((1, rows), table[4, h] * prev_i, jnp.int32) == 1
        use_n = jnp.full((1, rows), table[5, h] * next_i, jnp.int32) == 1
        m0, l0 = part_ml[0, h, 0:1, :], part_ml[0, h, 1:2, :]
        m1, l1 = part_ml[1, h, 0:1, :], part_ml[1, h, 1:2, :]
        ml_p, ml_n = part_ml[2, slot_p], part_ml[3, slot_n]
        m2 = jnp.where(use_p, ml_p[0:1], masked_score)
        m3 = jnp.where(use_n, ml_n[0:1], masked_score)
        l2 = jnp.where(use_p, ml_p[1:2], 0.0)
        l3 = jnp.where(use_n, ml_n[1:2], 0.0)
        top = jnp.maximum(jnp.maximum(m0, m1), jnp.maximum(m2, m3))
        f0 = jnp.exp2((m0 - top) * scale2)
        f1 = jnp.exp2((m1 - top) * scale2)
        f2 = jnp.exp2((m2 - top) * scale2)
        f3 = jnp.exp2((m3 - top) * scale2)
        total = l0 * f0 + l1 * f1 + l2 * f2 + l3 * f3
        share = 1.0 / total
        summed = (
            part_o[0, h] * (f0 * share)
            + part_o[1, h] * (f1 * share)
            + jnp.where(use_p, part_o[2, slot_p], 0.0) * (f2 * share)
            + jnp.where(use_n, part_o[3, slot_n], 0.0) * (f3 * share)
        )
        out_ref[:, cols(h)] = (summed.T * gate_ref[0:1, cols(h)]).astype(jnp.bfloat16)
        return 0

    lax.fori_loop(0, heads, finish, 0)

    def spread_land(d, _):
        source = lax.rem(pos + count - d, count)
        for kind in (0, 1):
            recv = (o_recv, s_recv)[kind]
            send = (o_send, s_send)[kind]
            pltpu.make_async_remote_copy(
                src_ref=send.at[source],
                dst_ref=recv.at[source],
                send_sem=as_sem.at[kind, d],
                recv_sem=ar_sem.at[kind, d],
                device_id=(grp, source),
                device_id_type=MESH,
            ).wait_recv()
        return 0

    lax.fori_loop(1, count, spread_land, 0)
    tops = s_recv[:, 0]
    top = jnp.max(tops, axis=0, keepdims=True)
    factors = jnp.exp2((tops - top) * scale2)
    total = jnp.sum(s_recv[:, 1] * factors, axis=0)
    factors = factors / jnp.where(total == 0.0, 1.0, total)[None]
    for h in range(heads):
        acc = jnp.zeros((tdev, width), jnp.float32)
        for d in range(count):
            acc = acc + o_recv[d, :, h * width : (h + 1) * width].astype(jnp.float32) * factors[
                d, :, h : h + 1
            ]
        gate = gate_ref[1:2, h * width : (h + 1) * width]
        tout_ref[:, h * width : (h + 1) * width] = (acc * gate).astype(jnp.bfloat16)

    for stage in range(stages):
        gather_sent(0, stage)
        gather_sent(1, stage)

    def spread_sent(d, _):
        target = lax.rem(pos + d, count)
        spread_copy(0, d, pos, target).wait_send()
        spread_copy(1, d, pos, target).wait_send()
        return 0

    lax.fori_loop(1, count, spread_sent, 0)

    def halo_sent(j, _):
        @pl.when(has_next)
        def _():
            halo_copy(0, j).wait_send()

        @pl.when(has_prev)
        def _():
            halo_copy(1, j).wait_send()

        return 0

    lax.fori_loop(0, slots, halo_sent, 0)


def head_table(window_offsets):
    heads = window_offsets.shape[0]
    flags = jnp.stack([window_offsets[:, 0] == -1, window_offsets[:, 1] == 1]).astype(jnp.int32)
    index = jnp.arange(heads, dtype=jnp.int32)
    before = (index[:, None] < index[None, :]).astype(jnp.int32)
    ranks = jnp.sum(flags[:, :, None] * before[None], axis=1)
    hit = (ranks[:, None, :] == index[None, :, None]).astype(jnp.int32) * flags[:, None, :]
    lists = jnp.sum(hit * index[None, None, :], axis=2)
    return jnp.concatenate([lists, ranks * flags, flags], axis=0), jnp.max(jnp.sum(flags, axis=1))


def fused_device(
    image_query,
    image_pairs,
    text_query,
    text_pairs,
    text_mask,
    window_offsets,
    timestep,
    gate_table,
):
    rows, width_all = image_query.shape
    heads = window_offsets.shape[0]
    width = width_all // heads
    count = lax.axis_size("rows")
    tdev = text_query.shape[0]
    text = tdev * count
    table, most = head_table(window_offsets)
    bias = jnp.broadcast_to(
        jnp.where(text_mask == 1, 0.0, masked_score).astype(jnp.float32)[:, None], (text, 128)
    )
    gate = lax.dynamic_index_in_dim(gate_table, timestep[0], 0, keepdims=False)
    scale2 = math.log2(math.e) / math.sqrt(width)
    vmem = pl.BlockSpec(memory_space=pltpu.VMEM)
    bf16, f32 = jnp.bfloat16, jnp.float32

    def build(slots, ident):
        return pl.pallas_call(
            functools.partial(joint_kernel, count, slots, heads, scale2),
            out_shape=(
                jax.ShapeDtypeStruct(image_query.shape, bf16),
                jax.ShapeDtypeStruct(text_query.shape, bf16),
            ),
            in_specs=[pl.BlockSpec(memory_space=pltpu.SMEM)] + [vmem] * 6,
            out_specs=(vmem, vmem),
            scratch_shapes=[
                pltpu.VMEM((heads, rows, width), bf16),
                pltpu.VMEM((heads, 2, rows, width), bf16),
                pltpu.VMEM((2, slots, 2, rows, width), bf16),
                pltpu.VMEM((2, slots, 2, rows, width), bf16),
                pltpu.VMEM((count, tdev, width_all), bf16),
                pltpu.VMEM((2, count, tdev, width_all), bf16),
                pltpu.VMEM((4, heads, width, rows), f32),
                pltpu.VMEM((4, heads, 8, rows), f32),
                pltpu.VMEM((2, 128, text), f32),
                pltpu.VMEM((count, tdev, width_all), bf16),
                pltpu.VMEM((count, tdev, width_all), bf16),
                pltpu.VMEM((count, 2, tdev, 128), f32),
                pltpu.VMEM((count, 2, tdev, 128), f32),
                pltpu.SemaphoreType.DMA((2, count)),
                pltpu.SemaphoreType.DMA((2, count)),
                pltpu.SemaphoreType.DMA((2, slots)),
                pltpu.SemaphoreType.DMA((2, slots)),
                pltpu.SemaphoreType.DMA((2, count)),
                pltpu.SemaphoreType.DMA((2, count)),
            ],
            compiler_params=pltpu.CompilerParams(
                collective_id=ident, has_side_effects=True, vmem_limit_bytes=56 << 20
            ),
        )

    args = (table, image_query, image_pairs, text_query, text_pairs, bias, gate)
    sizes = [cap for cap in CAPS if cap < heads] + [heads]
    branches = [build(slots, i) for i, slots in enumerate(sizes)]
    if len(branches) == 1:
        return branches[0](*args)
    which = sum((most > cap).astype(jnp.int32) for cap in sizes[:-1])
    return lax.switch(which, branches, *args)


def joint(*args):
    rows = args[0].shape[0]
    tdev = args[2].shape[0]
    heads = args[5].shape[0]
    count = lax.axis_size("rows")
    fits = rows == TILE and tdev % 16 == 0 and count & (count - 1) == 0 and heads <= 128
    if fits and count <= 32 and args[0].shape[1] == heads * 128:
        return fused_device(*args)
    return on_device(*args)


def solution(mesh):
    placed = (
        P(("groups", "rows"), None),
        P(None, ("groups", "rows"), None),
        P(("groups", "rows"), None),
        P(None, ("groups", "rows"), None),
        P("groups"),
        P(),
        P(),
        P(),
    )
    return jax.shard_map(
        joint,
        mesh=mesh,
        in_specs=placed,
        out_specs=(P(("groups", "rows"), None), P(("groups", "rows"), None)),
        check_vma=False,
    )
```

```python
import functools
import math

import jax
import jax.numpy as jnp
from jax import lax
from jax.experimental import pallas as pl
from jax.experimental.pallas import tpu as pltpu
from jax.sharding import PartitionSpec as P

TILE = 384


masked_score = -1e30


def extended_2(cells, sides, width):
    for axis, dim in sides:
        count = lax.axis_size(axis)
        ends = count - 1
        head = lax.slice_in_dim(cells, 0, width, axis=dim)
        tail = lax.slice_in_dim(cells, cells.shape[dim] - width, cells.shape[dim], axis=dim)
        cells = jnp.concatenate(
            [
                lax.ppermute(tail, axis, [(i, (i + 1) % count) for i in range(ends)]),
                cells,
                lax.ppermute(head, axis, [((i + 1) % count, i) for i in range(ends)]),
            ],
            axis=dim,
        )
    return cells


def attend_tiles(queries, key_rows, value_rows, allowed, scaling):
    scores = (
        jnp.einsum("tqhe,tkhe->tqhk", queries, key_rows, preferred_element_type=jnp.float32)
        * scaling
    )
    scores = jnp.where(allowed, scores, masked_score)
    maxima = jnp.max(scores, axis=-1)
    exponent = jnp.where(allowed, jnp.exp(scores - maxima[..., None]), 0.0)
    totals = jnp.sum(exponent, axis=-1)
    summed = jnp.einsum(
        "tqhk,tkhe->tqhe",
        exponent.astype(jnp.bfloat16),
        value_rows,
        preferred_element_type=jnp.float32,
    )
    return (maxima, totals, summed.astype(jnp.bfloat16))


def attend_rows(queries, key_rows, value_rows, allowed, scaling):
    scores = (
        jnp.einsum("qhe,khe->qhk", queries, key_rows, preferred_element_type=jnp.float32) * scaling
    )
    scores = jnp.where(allowed, scores, masked_score)
    maxima = jnp.max(scores, axis=-1)
    exponent = jnp.where(allowed, jnp.exp(scores - maxima[..., None]), 0.0)
    totals = jnp.sum(exponent, axis=-1)
    summed = jnp.einsum(
        "qhk,khe->qhe",
        exponent.astype(jnp.bfloat16),
        value_rows,
        preferred_element_type=jnp.float32,
    )
    return (maxima, totals, summed.astype(jnp.bfloat16))


def combine_groups(groups):
    largest = groups[0][0]
    for member in groups[1:]:
        largest = jnp.maximum(largest, member[0])
    totals = 0.0
    summed = 0.0
    for member in groups:
        factor = jnp.exp(member[0] - largest)
        totals = totals + member[1] * factor
        summed = summed + member[2].astype(jnp.float32) * factor[..., None]
    return summed / totals[..., None]


def on_device(
    image_query,
    image_pairs,
    text_query,
    text_pairs,
    text_mask,
    window_offsets,
    timestep,
    gate_table,
):
    rows_dev, width = image_query.shape
    tiles_dev = rows_dev // TILE
    head_count = window_offsets.shape[0]
    head_width = width // head_count
    scaling = 1.0 / math.sqrt(head_width)
    position = lax.axis_index("rows")
    tiles_all = tiles_dev * lax.axis_size("rows")
    first_tile = position * tiles_dev
    reach_back = window_offsets[:, 0]
    reach_ahead = window_offsets[:, 1]
    text_queries, text_gathered = (
        lax.all_gather(text_query, "rows", axis=0, tiled=True),
        lax.all_gather(text_pairs, "rows", axis=1, tiled=True),
    )
    text_keys = text_gathered[0].reshape(-1, head_count, head_width)
    text_values = text_gathered[1].reshape(-1, head_count, head_width)
    text_allowed = (text_mask == 1)[None, None, :]
    queries = image_query.reshape(tiles_dev, TILE, head_count, head_width)
    local_keys = image_pairs[0].reshape(tiles_dev, TILE, head_count, head_width)
    local_values = image_pairs[1].reshape(tiles_dev, TILE, head_count, head_width)

    def permitted(offset):
        target = first_tile + jnp.arange(tiles_dev, dtype=jnp.int32) + offset
        inside = (target >= 0) & (target < tiles_all)
        within = (reach_back <= offset) & (offset <= reach_ahead)
        return (inside[:, None] & within[None, :])[:, None, :, None]

    flat_queries = image_query.reshape(rows_dev, head_count, head_width)
    text_group = attend_rows(flat_queries, text_keys, text_values, text_allowed, scaling)
    text_group = (
        text_group[0].reshape(tiles_dev, TILE, head_count),
        text_group[1].reshape(tiles_dev, TILE, head_count),
        text_group[2].reshape(tiles_dev, TILE, head_count, head_width),
    )
    groups = [attend_tiles(queries, local_keys, local_values, permitted(0), scaling), text_group]
    extended = extended_2(image_pairs, (("rows", 1),), TILE)
    extended = extended.reshape(2, tiles_dev + 2, TILE, head_count, head_width)
    for offset in (-1, 1):
        groups.append(
            attend_tiles(
                queries,
                extended[0, 1 + offset : 1 + offset + tiles_dev],
                extended[1, 1 + offset : 1 + offset + tiles_dev],
                permitted(offset),
                scaling,
            )
        )
    gate_rows = lax.dynamic_index_in_dim(gate_table, timestep[0], 0, keepdims=False)
    attended = combine_groups(groups).reshape(rows_dev, width)
    image_out = (attended * gate_rows[0]).astype(jnp.bfloat16)
    text_flat = text_queries.reshape(-1, head_count, head_width)
    image_keys = image_pairs[0].reshape(rows_dev, head_count, head_width)
    image_values = image_pairs[1].reshape(rows_dev, head_count, head_width)
    every_key = jnp.ones((1, 1, rows_dev), dtype=bool)
    maxima, totals, summed = attend_rows(text_flat, image_keys, image_values, every_key, scaling)
    text_dev = text_query.shape[0]
    text_start = position * text_dev
    global_max = lax.pmax(maxima, "rows")
    factor = jnp.exp(maxima - global_max)
    scaled_summed = summed.astype(jnp.float32) * factor[..., None]
    scaled_totals = totals * factor
    whole_summed, whole_totals = lax.psum((scaled_summed, scaled_totals), "rows")
    shared_summed = lax.dynamic_slice_in_dim(whole_summed, text_start, text_dev, 0)
    shared_totals = lax.dynamic_slice_in_dim(whole_totals, text_start, text_dev, 0)
    remote = (
        lax.dynamic_slice_in_dim(global_max, text_start, text_dev, 0),
        shared_totals,
        shared_summed,
    )
    own_rows = text_query.reshape(text_dev, head_count, head_width)
    own_text = attend_rows(own_rows, text_keys, text_values, text_allowed, scaling)
    text_attended = combine_groups([remote, own_text]).reshape(text_dev, width)
    text_out = (text_attended * gate_rows[1]).astype(jnp.bfloat16)
    return (image_out, text_out)


CAPS = (10, 12)
LEAD = 2
MESH = pl.DeviceIdType.MESH


def flipped(pos, bits):
    out = pos
    bit = 1
    while bit <= bits:
        if bits & bit:
            out = out + bit - 2 * bit * ((pos // bit) % 2)
        bit *= 2
    return out


def stage_bits(count):
    bits = []
    bit = count // 2
    while bit >= 1:
        bits.append(bit)
        bit //= 2
    if len(bits) == 4:
        bits = [bits[0], bits[2], bits[1], bits[3]]
    return bits


def fold_bits(count):
    bits = stage_bits(count)
    return bits[::-1]


def joint_kernel(
    count,
    slots,
    heads,
    scale2,
    table,
    q_ref,
    pairs_ref,
    tq_ref,
    tp_ref,
    bias_ref,
    gate_ref,
    out_ref,
    tout_ref,
    hq,
    hkv,
    packed,
    landed,
    tq_all,
    tkv_all,
    part_o,
    part_ml,
    stat,
    o_send,
    o_recv,
    s_send,
    s_recv,
    gs_sem,
    gr_sem,
    hs_sem,
    hr_sem,
    as_sem,
    ar_sem,
):
    pos = lax.axis_index("rows")
    grp = lax.axis_index("groups")
    rows = q_ref.shape[0]
    tdev = tq_ref.shape[0]
    text = count * tdev
    width = q_ref.shape[1] // heads

    barrier = pltpu.get_barrier_semaphore()

    def greet(d, _):
        pl.semaphore_signal(
            barrier, inc=1, device_id=(grp, lax.rem(pos + d, count)), device_id_type=MESH
        )
        return 0

    lax.fori_loop(1, count, greet, 0)
    pl.semaphore_wait(barrier, count - 1)

    def cols(h):
        return pl.ds(pl.multiple_of(h * width, width), width)

    bits = stage_bits(count)
    refs = (tq_all, tkv_all)

    def gather_copy(kind, number, block, partner):
        ref = tq_all.at[block] if kind == 0 else tkv_all.at[:, block]
        return pltpu.make_async_remote_copy(
            src_ref=ref,
            dst_ref=ref,
            send_sem=gs_sem.at[kind, number],
            recv_sem=gr_sem.at[kind, number],
            device_id=(grp, partner),
            device_id_type=MESH,
        )

    plan = []
    offsets = [0]
    number = 0
    for bit in bits:
        stage = []
        for off in offsets:
            stage.append((number, off, bit))
            number += 1
        plan.append(stage)
        offsets = offsets + [off ^ bit for off in offsets]

    def gather_start(kind, stage):
        for num, off, bit in plan[stage]:
            gather_copy(kind, num, flipped(pos, off), flipped(pos, bit)).start()

    def gather_land(kind, stage):
        for num, off, bit in plan[stage]:
            gather_copy(kind, num, flipped(pos, off ^ bit), flipped(pos, bit)).wait_recv()

    def gather_sent(kind, stage):
        for num, off, bit in plan[stage]:
            gather_copy(kind, num, flipped(pos, off), flipped(pos, bit)).wait_send()

    tq_all[pos] = tq_ref[...]
    tkv_all[:, pos] = tp_ref[...]
    gather_start(0, 0)
    gather_start(1, 0)

    def halo_copy(side, j):
        partner = pos + 1 if side == 0 else pos - 1
        return pltpu.make_async_remote_copy(
            src_ref=packed.at[side, j],
            dst_ref=landed.at[side, j],
            send_sem=hs_sem.at[side, j],
            recv_sem=hr_sem.at[side, j],
            device_id=(grp, partner),
            device_id_type=MESH,
        )

    has_prev = pos > 0
    has_next = pos < count - 1

    for h in range(heads):
        at = slice(h * width, (h + 1) * width)
        hkv[h] = pairs_ref[:, :, at]
        hq[h] = q_ref[:, at]

    def pack(j, _):
        @pl.when(has_next)
        def _():
            h = table[0, j]
            packed[0, j] = hkv[h]
            halo_copy(0, j).start()

        @pl.when(has_prev)
        def _():
            h = table[1, j]
            packed[1, j] = hkv[h]
            halo_copy(1, j).start()

        return 0


    def partial(keys, values, queries, bias):
        scores = lax.dot_general(
            keys, queries, (((1,), (1,)), ((), ())), preferred_element_type=jnp.float32
        )
        if bias is not None:
            scores = scores + bias
        top = jnp.max(scores, axis=0, keepdims=True)
        weights = jnp.exp2((scores - top) * scale2)
        total = jnp.sum(weights, axis=0, keepdims=True)
        summed = lax.dot_general(
            values,
            weights.astype(jnp.bfloat16),
            (((0,), (0,)), ((), ())),
            preferred_element_type=jnp.float32,
        )
        return top, total, summed

    def keep(kind, j, result):
        top, total, summed = result
        part_o[kind, j] = summed
        part_ml[kind, j, 0:1, :] = top
        part_ml[kind, j, 1:2, :] = total

    def pairwise(first, last, head):
        def two(i, _):
            h = first + 2 * i
            results = (head(h), head(h + 1))
            for k in range(2):
                for kind, j, result in results[k]:
                    keep(kind, j, result)
            return 0

        lax.fori_loop(0, (last - first) // 2, two, 0)

    def local_head(h):
        return [(0, h, partial(hkv[h, 0], hkv[h, 1], hq[h], None))]

    stages = len(bits)
    done, begun = 0, 0
    for stage in range(stages):
        ahead = min(slots, LEAD * (stage + 1))
        lax.fori_loop(begun, ahead, pack, 0)
        begun = ahead
        upto = heads * (stage + 1) // stages
        pairwise(done, upto, local_head)
        done = upto
        for kind in (0, 1):
            gather_land(kind, stage)
            if stage + 1 < stages:
                gather_start(kind, stage + 1)
    lax.fori_loop(begun, slots, pack, 0)

    stat[...] = jnp.zeros_like(stat)
    own_bias = bias_ref[pl.ds(pl.multiple_of(pos * tdev, tdev), tdev), 0:1]
    slab_bias = jnp.concatenate([jnp.zeros((rows, 1), jnp.float32), own_bias], axis=0)

    def text_head(h):
        keys = jnp.concatenate([hkv[h, 0], tp_ref[0, :, cols(h)]], axis=0)
        values = jnp.concatenate([hkv[h, 1], tp_ref[1, :, cols(h)]], axis=0)
        queries = tq_all[:, :, cols(h)].reshape(text, width)
        return partial(keys, values, queries, slab_bias)

    def text_pair(i, _):
        results = (text_head(2 * i), text_head(2 * i + 1))
        for k in range(2):
            h = 2 * i + k
            top, total, summed = results[k]
            stat[0, pl.ds(h, 1), :] = top
            stat[1, pl.ds(h, 1), :] = total
            o_send[:, :, cols(h)] = summed.T.astype(jnp.bfloat16).reshape(count, tdev, width)
        return 0

    lax.fori_loop(0, heads // 2, text_pair, 0)
    s_send[:, 0] = stat[0].T.reshape(count, tdev, 128)
    s_send[:, 1] = stat[1].T.reshape(count, tdev, 128)

    halving = fold_bits(count)
    folds = []
    number = 0
    for k in range(len(halving)):
        spans = [0]
        for bit in halving[k + 1 :]:
            spans = spans + [off ^ bit for off in spans]
        folds.append([(number + i, off, halving[k]) for i, off in enumerate(spans)])
        number += len(spans)

    def fold_copy(kind, num, off, bit):
        send, recv = ((o_send, o_recv), (s_send, s_recv))[kind]
        return pltpu.make_async_remote_copy(
            src_ref=send.at[flipped(pos, off ^ bit)],
            dst_ref=recv.at[num],
            send_sem=as_sem.at[kind, num],
            recv_sem=ar_sem.at[kind, num],
            device_id=(grp, flipped(pos, bit)),
            device_id_type=MESH,
        )

    def fold_start(k):
        for num, off, bit in folds[k]:
            fold_copy(0, num, off, bit).start()
            fold_copy(1, num, off, bit).start()

    def fold_merge(k):
        for num, off, bit in folds[k]:
            fold_copy(0, num, off, bit).wait_recv()
            fold_copy(1, num, off, bit).wait_recv()
            block = flipped(pos, off)
            m0, m1 = s_send[block, 0], s_recv[num, 0]
            top = jnp.maximum(m0, m1)
            f0 = jnp.exp2((m0 - top) * scale2)
            f1 = jnp.exp2((m1 - top) * scale2)
            s_send[block, 0] = top
            s_send[block, 1] = s_send[block, 1] * f0 + s_recv[num, 1] * f1
            for h in range(heads):
                at = slice(h * width, (h + 1) * width)
                o_send[block, :, at] = (
                    o_send[block, :, at].astype(jnp.float32) * f0[:, h : h + 1]
                    + o_recv[num, :, at].astype(jnp.float32) * f1[:, h : h + 1]
                ).astype(jnp.bfloat16)

    fold_start(0)

    def image_text(h):
        keys = tkv_all[0, :, :, cols(h)].reshape(text, width)
        values = tkv_all[1, :, :, cols(h)].reshape(text, width)
        return [(1, h, partial(keys, values, hq[h], bias_ref[:, 0:1]))]

    def halo_head(j, _):
        @pl.when(has_prev)
        def _():
            halo_copy(0, j).wait_recv()

        @pl.when(has_next)
        def _():
            halo_copy(1, j).wait_recv()

        before = partial(landed[0, j, 0], landed[0, j, 1], hq[table[0, j]], None)
        after = partial(landed[1, j, 0], landed[1, j, 1], hq[table[1, j]], None)
        keep(2, j, before)
        keep(3, j, after)
        return 0

    last = len(folds)
    done, seen = 0, 0
    for k in range(last):
        if k < last // 2:
            upto = heads * (k + 1) // (last // 2)
            pairwise(done, upto, image_text)
            done = upto
        else:
            upto = slots * (k + 1 - last // 2) // (last - last // 2 + 1)
            lax.fori_loop(seen, upto, halo_head, 0)
            seen = upto
        fold_merge(k)
        if k + 1 < last:
            fold_start(k + 1)
    lax.fori_loop(seen, slots, halo_head, 0)

    prev_i = jnp.where(has_prev, 1, 0)
    next_i = jnp.where(has_next, 1, 0)

    def finish(h, _):
        slot_p, slot_n = table[2, h], table[3, h]
        use_p = jnp.full((1, rows), table[4, h] * prev_i, jnp.int32) == 1
        use_n = jnp.full((1, rows), table[5, h] * next_i, jnp.int32) == 1
        m0, l0 = part_ml[0, h, 0:1, :], part_ml[0, h, 1:2, :]
        m1, l1 = part_ml[1, h, 0:1, :], part_ml[1, h, 1:2, :]
        ml_p, ml_n = part_ml[2, slot_p], part_ml[3, slot_n]
        m2 = jnp.where(use_p, ml_p[0:1], masked_score)
        m3 = jnp.where(use_n, ml_n[0:1], masked_score)
        l2 = jnp.where(use_p, ml_p[1:2], 0.0)
        l3 = jnp.where(use_n, ml_n[1:2], 0.0)
        top = jnp.maximum(jnp.maximum(m0, m1), jnp.maximum(m2, m3))
        f0 = jnp.exp2((m0 - top) * scale2)
        f1 = jnp.exp2((m1 - top) * scale2)
        f2 = jnp.exp2((m2 - top) * scale2)
        f3 = jnp.exp2((m3 - top) * scale2)
        total = l0 * f0 + l1 * f1 + l2 * f2 + l3 * f3
        share = 1.0 / total
        summed = (
            part_o[0, h] * (f0 * share)
            + part_o[1, h] * (f1 * share)
            + jnp.where(use_p, part_o[2, slot_p], 0.0) * (f2 * share)
            + jnp.where(use_n, part_o[3, slot_n], 0.0) * (f3 * share)
        )
        out_ref[:, cols(h)] = (summed.T * gate_ref[0:1, cols(h)]).astype(jnp.bfloat16)
        return 0

    lax.fori_loop(0, heads, finish, 0)

    share = 1.0 / s_send[pos, 1]
    for h in range(heads):
        at = slice(h * width, (h + 1) * width)
        rescaled = o_send[pos, :, at].astype(jnp.float32) * share[:, h : h + 1]
        tout_ref[:, at] = (rescaled * gate_ref[1:2, at]).astype(jnp.bfloat16)

    for stage in range(stages):
        gather_sent(0, stage)
        gather_sent(1, stage)

    for stage in folds:
        for num, off, bit in stage:
            fold_copy(0, num, off, bit).wait_send()
            fold_copy(1, num, off, bit).wait_send()

    def halo_sent(j, _):
        @pl.when(has_next)
        def _():
            halo_copy(0, j).wait_send()

        @pl.when(has_prev)
        def _():
            halo_copy(1, j).wait_send()

        return 0

    lax.fori_loop(0, slots, halo_sent, 0)


def head_table(window_offsets):
    heads = window_offsets.shape[0]
    flags = jnp.stack([window_offsets[:, 0] == -1, window_offsets[:, 1] == 1]).astype(jnp.int32)
    index = jnp.arange(heads, dtype=jnp.int32)
    before = (index[:, None] < index[None, :]).astype(jnp.int32)
    ranks = jnp.sum(flags[:, :, None] * before[None], axis=1)
    hit = (ranks[:, None, :] == index[None, :, None]).astype(jnp.int32) * flags[:, None, :]
    lists = jnp.sum(hit * index[None, None, :], axis=2)
    return jnp.concatenate([lists, ranks * flags, flags], axis=0), jnp.max(jnp.sum(flags, axis=1))


def fused_device(
    image_query,
    image_pairs,
    text_query,
    text_pairs,
    text_mask,
    window_offsets,
    timestep,
    gate_table,
):
    rows, width_all = image_query.shape
    heads = window_offsets.shape[0]
    width = width_all // heads
    count = lax.axis_size("rows")
    tdev = text_query.shape[0]
    text = tdev * count
    table, most = head_table(window_offsets)
    bias = jnp.broadcast_to(
        jnp.where(text_mask == 1, 0.0, masked_score).astype(jnp.float32)[:, None], (text, 128)
    )
    gate = lax.dynamic_index_in_dim(gate_table, timestep[0], 0, keepdims=False)
    scale2 = math.log2(math.e) / math.sqrt(width)
    vmem = pl.BlockSpec(memory_space=pltpu.VMEM)
    bf16, f32 = jnp.bfloat16, jnp.float32

    def build(slots, ident):
        return pl.pallas_call(
            functools.partial(joint_kernel, count, slots, heads, scale2),
            out_shape=(
                jax.ShapeDtypeStruct(image_query.shape, bf16),
                jax.ShapeDtypeStruct(text_query.shape, bf16),
            ),
            in_specs=[pl.BlockSpec(memory_space=pltpu.SMEM)] + [vmem] * 6,
            out_specs=(vmem, vmem),
            scratch_shapes=[
                pltpu.VMEM((heads, rows, width), bf16),
                pltpu.VMEM((heads, 2, rows, width), bf16),
                pltpu.VMEM((2, slots, 2, rows, width), bf16),
                pltpu.VMEM((2, slots, 2, rows, width), bf16),
                pltpu.VMEM((count, tdev, width_all), bf16),
                pltpu.VMEM((2, count, tdev, width_all), bf16),
                pltpu.VMEM((4, heads, width, rows), f32),
                pltpu.VMEM((4, heads, 8, rows), f32),
                pltpu.VMEM((2, 128, text), f32),
                pltpu.VMEM((count, tdev, width_all), bf16),
                pltpu.VMEM((count, tdev, width_all), bf16),
                pltpu.VMEM((count, 2, tdev, 128), f32),
                pltpu.VMEM((count, 2, tdev, 128), f32),
                pltpu.SemaphoreType.DMA((2, count)),
                pltpu.SemaphoreType.DMA((2, count)),
                pltpu.SemaphoreType.DMA((2, slots)),
                pltpu.SemaphoreType.DMA((2, slots)),
                pltpu.SemaphoreType.DMA((2, count)),
                pltpu.SemaphoreType.DMA((2, count)),
            ],
            compiler_params=pltpu.CompilerParams(
                collective_id=ident, has_side_effects=True, vmem_limit_bytes=56 << 20
            ),
        )

    args = (table, image_query, image_pairs, text_query, text_pairs, bias, gate)
    sizes = [cap for cap in CAPS if cap < heads] + [heads]
    branches = [build(slots, i) for i, slots in enumerate(sizes)]
    if len(branches) == 1:
        return branches[0](*args)
    which = sum((most > cap).astype(jnp.int32) for cap in sizes[:-1])
    return lax.switch(which, branches, *args)


def joint(*args):
    rows = args[0].shape[0]
    tdev = args[2].shape[0]
    heads = args[5].shape[0]
    count = lax.axis_size("rows")
    fits = rows == TILE and tdev % 16 == 0 and count & (count - 1) == 0 and heads <= 128
    if fits and count <= 32 and args[0].shape[1] == heads * 128:
        return fused_device(*args)
    return on_device(*args)


def solution(mesh):
    placed = (
        P(("groups", "rows"), None),
        P(None, ("groups", "rows"), None),
        P(("groups", "rows"), None),
        P(None, ("groups", "rows"), None),
        P("groups"),
        P(),
        P(),
        P(),
    )
    return jax.shard_map(
        joint,
        mesh=mesh,
        in_specs=placed,
        out_specs=(P(("groups", "rows"), None), P(("groups", "rows"), None)),
        check_vma=False,
    )
```
